32 devices in a mesh: pole: 2 (over x), prow: 4 (over y, core), pcol: 4 (over z).
Axes of the slice: x: 2, y: 2, z: 4, core: 2. Of those that a mesh axis runs over, the one named last changes fastest.
Arguments:
- root_inverse: float32 [6144, 3072], P(('pole', 'prow'), 'pcol'), parts along dimension 0, may hold values from -6 to 6, as said below
- lower_blocks: float32 [6144, 1024], P(('pole', 'pcol'), 'prow'), parts along dimension 0, may hold values from -0.109375 to 0.109375
- block_pattern: int32 [12, 4], replicated, may hold values 0 or 1
- diag_inverse: float32 [8, 256, 256], P(('pole', 'pcol'), 'prow'), parts along dimension 0, may hold values from -6 to 6, as said below
Outputs:
- selected: float32 [6144, 1024], P(('pole', 'prow'), 'pcol'), parts along dimension 0
- diagonal_blocks: float32 [8, 256, 256], P(('pole', 'pcol'), 'prow'), parts along dimension 0
The draws below stay inside these ranges and needn't reach their ends.
There are 2 independent parts, one for each index of `pole`. The reference program is written for one: setup_inputs(seed, part) draws one part's arguments, and reference() takes and returns one part's arrays. A program takes and returns all parts, laid end to end along the dimension named above; an argument that names none is the same for every part. Nothing has to cross between parts.
Inputs may be any that keep to these rules, and one draw needn't show every extreme that they name: `root_inverse`: symmetric. `diag_inverse`: each block symmetric.
All inputs are finite; a program needn't handle non-finite values.
Results may differ from the reference program's by a relative error of at most 0.000071.
Values sent between devices are 32-bit elements; how exact they have to be, the bound alone decides.
A program may use at most 128 MiB of HBM per device.

```python
import jax
import jax.numpy as jnp
from jax import lax

B = 256
NBR = 12
NR = 3072
S = 4


def draw_root_inverse(key, part):
    key = jax.random.fold_in(key, 11)
    values = jax.random.normal(key, (NR, NR), jnp.float32)
    return jnp.clip((values + values.T) * 0.7071, -6.0, 6.0)


def draw_diag_inverse(key, part):
    key = jax.random.fold_in(key, 23)
    values = jax.random.normal(key, (S, B, B), jnp.float32)
    return jnp.clip((values + jnp.swapaxes(values, 1, 2)) * 0.7071, -6.0, 6.0)


def touch_ends(result, key, low, high):
    extent = result.shape
    place = [jax.random.randint(jax.random.fold_in(key, axis), (), 0, extent[axis]) for axis in range(len(extent))]
    result = result.at[tuple(place)].set(low)
    longest = extent.index(max(extent))
    place[longest] = (place[longest] + 1) % extent[longest]
    return result.at[tuple(place)].set(high)


def block_levels(rng, dims, shards, low, top_value):
    level = 1.0
    for dim, shards_of in shards:
        heights = jax.random.uniform(jax.random.fold_in(jax.random.fold_in(rng, 6), dim), (shards_of,), jnp.float32, low / len(shards), top_value / len(shards))
        level = level * jnp.repeat(jnp.exp(heights), dims[dim] // shards_of).reshape((-1,) + (1,) * (len(dims) - 1 - dim))
    return level


def bell_draw(key, shape, scale, most, shards=(), dtype=jnp.bfloat16):
    entries = jax.random.normal(key, shape, jnp.float32) * scale
    if len(shards) > 0:
        entries = block_levels(key, shape, shards, -0.22, 0.18) * entries
    return jnp.clip(entries, min=-most, max=most).astype(dtype)


def setup_inputs(seed: int = 0, part: int = 0) -> dict:
    keys = jax.random.split(jax.random.key(seed), 5)
    own_keys = jax.random.split(jax.random.fold_in(keys[4], part), 5)
    root_inverse = draw_root_inverse(jax.random.fold_in(jax.random.fold_in(keys[4], part), 71), part)
    lower_blocks = bell_draw(own_keys[1], (NR, S * B), NR ** -0.5, 0.109375, ((0, 4), (1, 4)), jnp.float32)
    block_pattern = touch_ends((jax.random.randint(keys[2], (NBR, S), 0, 2) < 1).astype(jnp.int32), jax.random.fold_in(keys[2], 1), 0, 1)
    diag_inverse = draw_diag_inverse(jax.random.fold_in(jax.random.fold_in(keys[4], part), 71), part)
    return {"root_inverse": root_inverse, "lower_blocks": lower_blocks, "block_pattern": block_pattern, "diag_inverse": diag_inverse}


def reference(root_inverse, lower_blocks, block_pattern, diag_inverse):
    block_mask = jnp.repeat(jnp.repeat(block_pattern.astype(jnp.float32), B, axis=0), B, axis=1)
    masked = lower_blocks * block_mask
    selected = -jnp.dot(root_inverse, masked, precision=lax.Precision.HIGHEST, preferred_element_type=jnp.float32)
    lower_split = masked.reshape(NR, S, B)
    upper_split = selected.reshape(NR, S, B)
    correction = jnp.einsum("isa,isb->sab", lower_split, upper_split, precision=lax.Precision.HIGHEST)
    return selected, diag_inverse - correction
```

```python
import functools

import jax
import jax.numpy as jnp
from jax import lax
from jax.experimental import pallas as pl
from jax.experimental.pallas import tpu as pltpu
from jax.sharding import PartitionSpec as P

B = 256
MESH = pl.DeviceIdType.MESH


def split(value):
    high = value.astype(jnp.bfloat16)
    return high, (value - high.astype(jnp.float32)).astype(jnp.bfloat16)


def dot3(ahi, alo, bhi, blo):
    dot = functools.partial(jnp.dot, preferred_element_type=jnp.float32)
    return dot(ahi, bhi) + (dot(ahi, blo) + dot(alo, bhi))


def kernel(
    PR, PC, H,
    pattern, root, lower, diag, sel, out,
    G, part, recv, rhi, rlo, lhi, llo, X, xthi, xtlo, D, E,
    ygs, ygr, fws, fwr, chs, chr_, xs, xr, ds_, dr,
):
    x = lax.axis_index("pole")
    p = lax.axis_index("prow")
    c = lax.axis_index("pcol")
    Y = PR // 2
    q = PR // PC if PR > PC else 1
    y, core = p // 2, p % 2
    mate = y * 2 + (1 - core)
    local_rows, local_cols = lower.shape
    panel = root.shape[0]
    hr = panel // H
    ratio = local_rows // panel
    pc = p // ratio
    row_off = pl.multiple_of(p % ratio * panel, panel)

    def remote(src, dst, ss, rs, pp, cc):
        return pltpu.make_async_remote_copy(
            src_ref=src, dst_ref=dst, send_sem=ss, recv_sem=rs,
            device_id=(x, pp, cc), device_id_type=MESH,
        )

    barrier = pltpu.get_barrier_semaphore()
    for t in range(1, PR):
        pl.semaphore_signal(barrier, inc=1, device_id=(x, (p + t) % PR, c), device_id_type=MESH)
    for t in range(1, PC):
        pl.semaphore_signal(barrier, inc=1, device_id=(x, p, (c + t) % PC), device_id_type=MESH)

    supernode = p * local_cols // B
    for r in range(local_rows // B):
        keep = pattern[c * (local_rows // B) + r, supernode].astype(jnp.float32)
        G[p, r * B:(r + 1) * B, :] = lower[r * B:(r + 1) * B, :] * keep
    pl.semaphore_wait(barrier, PR + PC - 2)

    def y_copy(t):
        return remote(G.at[p], G.at[p], ygs.at[t], ygr.at[t], (y + t) % Y * 2 + core, c)

    def forward(yy):
        b = yy * 2 + core
        return remote(G.at[b], G.at[b], fws.at[yy], fwr.at[yy], mate, c)

    for t in range(1, Y):
        y_copy(t).start()
    forward(y).start()

    def split_root(h, carry):
        rows = pl.ds(pl.multiple_of(h * hr, hr), hr)
        rhi[rows, :], rlo[rows, :] = split(root[rows, :])
        return carry

    lax.fori_loop(0, H, split_root, 0)

    def chain(u, h):
        j = u // q
        rows = pl.ds(pl.multiple_of(h * hr, hr), hr)
        target = jnp.where(j > c, c + 1, c - 1)
        slot = jnp.where((j < c) & (j == c - 1), PR + u % q, u)
        return remote(
            part.at[u, rows], recv.at[slot, rows], chs.at[u, h], chr_.at[slot, h], p, target
        )

    def arrive(slot, h):
        rows = pl.ds(pl.multiple_of(h * hr, hr), hr)
        remote(
            recv.at[slot, rows], recv.at[slot, rows], chs.at[0, h], chr_.at[slot, h], p, c
        ).wait_recv()

    def x_copy(u):
        return remote(
            G.at[u, pl.ds(row_off, panel)], X.at[u % q], xs.at[u], xr.at[u % q], p, u // q
        )

    def phase(t, carry):
        yy = (y + Y - t) % Y

        @pl.when(t > 0)
        def _():
            remote(G.at[p], G.at[yy * 2 + core], ygs.at[t], ygr.at[t], p, c).wait_recv()
            forward(yy).start()

        other = yy * 2 + (1 - core)
        remote(G.at[other], G.at[other], fws.at[yy], fwr.at[yy], p, c).wait_recv()
        for i in range(2):
            u = yy * 2 + i

            @pl.when((c == pc) & (u // q != c))
            def _():
                x_copy(u).start()

            lhi[i], llo[i] = split(G[u])

        def chunk(h, inner):
            rows = pl.ds(pl.multiple_of(h * hr, hr), hr)
            for i in range(2):
                u = yy * 2 + i
                j = u // q
                part[u, rows, :] = dot3(rhi[rows, :], rlo[rows, :], lhi[i], llo[i])

                @pl.when(((j > c) & (c > 0)) | ((j < c) & (c < PC - 1)))
                def _():
                    arrive(u, h)
                    part[u, rows, :] += recv[u, rows, :]

                @pl.when(j != c)
                def _():
                    chain(u, h).start()

            return inner

        lax.fori_loop(0, H, chunk, 0)
        return carry

    lax.fori_loop(0, Y, phase, 0)

    for i in range(q):
        @pl.when(c == pc)
        def _():
            X[i] = G[c * q + i, pl.ds(row_off, panel), :]

        @pl.when(c != pc)
        def _():
            remote(X.at[i], X.at[i], xs.at[0], xr.at[i], p, c).wait_recv()

        cols = slice(i * local_cols, (i + 1) * local_cols)
        xthi[cols, :], xtlo[cols, :] = split(X[i].T)

    D[...] = jnp.zeros_like(D)
    for h in range(H):
        rows = slice(h * hr, (h + 1) * hr)
        for i in range(q):
            u = c * q + i

            @pl.when(c > 0)
            def _():
                arrive(u, h)
                part[u, rows, :] += recv[u, rows, :]

            @pl.when(c < PC - 1)
            def _():
                arrive(PR + i, h)
                part[u, rows, :] += recv[PR + i, rows, :]

            cols = slice(i * local_cols, (i + 1) * local_cols)
            done = -part[u, rows, :]
            sel[rows, cols] = done
            D[:, cols] -= dot3(xthi[:, rows], xtlo[:, rows], *split(done))

    share = out.shape[1]

    def d_copy(t):
        pp = (p + t) % PR
        return remote(
            D.at[pl.ds(pl.multiple_of(pp * share, share), share)], E.at[t], ds_.at[t], dr.at[t], pp, c
        )

    for t in range(1, PR):
        d_copy(t).start()
    out[0] = diag[0] + D[pl.ds(pl.multiple_of(p * share, share), share), :]
    for t in range(1, PR):
        d_copy(t).wait_recv()
        out[0] += E[t]

    for t in range(1, PR):
        d_copy(t).wait_send()
    for t in range(1, Y):
        y_copy(t).wait_send()

    def drain_forward(yy, carry):
        forward(yy).wait_send()
        return carry

    lax.fori_loop(0, Y, drain_forward, 0)

    def drain(u, carry):
        @pl.when((c == pc) & (u // q != c))
        def _():
            x_copy(u).wait_send()

        @pl.when(u // q != c)
        def _():
            def one(h, inner):
                chain(u, h).wait_send()
                return inner

            lax.fori_loop(0, H, one, 0)

        return carry

    lax.fori_loop(0, PR, drain, 0)


def on_device(PR, PC, root_inverse, lower_blocks, block_pattern, diag_inverse):
    panel, depth = root_inverse.shape
    local_rows, local_cols = lower_blocks.shape
    H = panel // 128
    Y = PR // 2
    owned = local_cols * PR // PC
    q = owned // local_cols
    f32, bf16 = jnp.float32, jnp.bfloat16
    dma = pltpu.SemaphoreType.DMA
    vmem = pl.BlockSpec(memory_space=pltpu.VMEM)
    flops = 6 * panel * depth * local_cols * PR
    return pl.pallas_call(
        functools.partial(kernel, PR, PC, H),
        out_shape=(
            jax.ShapeDtypeStruct((panel, owned), f32),
            jax.ShapeDtypeStruct(diag_inverse.shape, f32),
        ),
        in_specs=[pl.BlockSpec(memory_space=pltpu.SMEM), vmem, vmem, vmem],
        out_specs=(vmem, vmem),
        scratch_shapes=[
            pltpu.VMEM((PR, local_rows, local_cols), f32),
            pltpu.VMEM((PR, panel, local_cols), f32),
            pltpu.VMEM((PR + q, panel, local_cols), f32),
            pltpu.VMEM((panel, depth), bf16),
            pltpu.VMEM((panel, depth), bf16),
            pltpu.VMEM((2, local_rows, local_cols), bf16),
            pltpu.VMEM((2, local_rows, local_cols), bf16),
            pltpu.VMEM((q, panel, local_cols), f32),
            pltpu.VMEM((owned, panel), bf16),
            pltpu.VMEM((owned, panel), bf16),
            pltpu.VMEM((owned, owned), f32),
            pltpu.VMEM((PR,) + diag_inverse.shape[1:], f32),
            dma((Y,)), dma((Y,)), dma((Y,)), dma((Y,)),
            dma((PR, H)), dma((PR + q, H)),
            dma((PR,)), dma((q,)), dma((PR,)), dma((PR,)),
        ],
        compiler_params=pltpu.CompilerParams(
            collective_id=0, has_side_effects=True, vmem_limit_bytes=56 * 1024 * 1024
        ),
        cost_estimate=pl.CostEstimate(flops=flops, bytes_accessed=8 * panel * depth, transcendentals=0),
    )(block_pattern, root_inverse, lower_blocks, diag_inverse)


def solution(mesh):
    placed = (
        P(("pole", "prow"), "pcol"),
        P(("pole", "pcol"), "prow"),
        P(),
        P(("pole", "pcol"), "prow", None),
    )
    return jax.shard_map(
        functools.partial(on_device, mesh.shape["prow"], mesh.shape["pcol"]),
        mesh=mesh,
        in_specs=placed,
        out_specs=(P(("pole", "prow"), "pcol"), P(("pole", "pcol"), "prow", None)),
        check_vma=False,
    )
```

```python
import functools

import jax
import jax.numpy as jnp
from jax import lax
from jax.experimental import pallas as pl
from jax.experimental.pallas import tpu as pltpu
from jax.sharding import PartitionSpec as P

B = 256
MESH = pl.DeviceIdType.MESH


def split(value):
    high = value.astype(jnp.bfloat16)
    return high, (value - high.astype(jnp.float32)).astype(jnp.bfloat16)


def dot3(ahi, alo, bhi, blo):
    dot = functools.partial(jnp.dot, preferred_element_type=jnp.float32)
    return dot(ahi, bhi) + (dot(ahi, blo) + dot(alo, bhi))


def kernel(
    PR, PC, H,
    pattern, root, lower, diag, sel, out,
    G, part, recv, rhi, rlo, lhi, llo, X, xthi, xtlo, D, E,
    ygs, ygr, fws, fwr, chs, chr_, xs, xr, ds_, dr,
):
    x = lax.axis_index("pole")
    p = lax.axis_index("prow")
    c = lax.axis_index("pcol")
    Y = PR // 2
    q = PR // PC if PR > PC else 1
    y, core = p // 2, p % 2
    mate = y * 2 + (1 - core)
    local_rows, local_cols = lower.shape
    panel = root.shape[0]
    hr = panel // H
    ratio = local_rows // panel
    pc = p // ratio
    row_off = pl.multiple_of(p % ratio * panel, panel)

    def remote(src, dst, ss, rs, pp, cc):
        return pltpu.make_async_remote_copy(
            src_ref=src, dst_ref=dst, send_sem=ss, recv_sem=rs,
            device_id=(x, pp, cc), device_id_type=MESH,
        )

    barrier = pltpu.get_barrier_semaphore()
    for t in range(1, PR):
        pl.semaphore_signal(barrier, inc=1, device_id=(x, (p + t) % PR, c), device_id_type=MESH)
    for t in range(1, PC):
        pl.semaphore_signal(barrier, inc=1, device_id=(x, p, (c + t) % PC), device_id_type=MESH)

    def away(r):
        return (c * ratio + r != p) | (p // q != c)

    for r in range(ratio):
        @pl.when(away(r))
        def _():
            pl.semaphore_signal(
                barrier, inc=1, device_id=(x, c * ratio + r, p // q), device_id_type=MESH
            )

    supernode = p * local_cols // B
    for r in range(local_rows // B):
        keep = pattern[c * (local_rows // B) + r, supernode].astype(jnp.float32)
        G[p, r * B:(r + 1) * B, :] = lower[r * B:(r + 1) * B, :] * keep
    extra = sum(jnp.where(away(r), 1, 0) for r in range(ratio))
    pl.semaphore_wait(barrier, PR + PC - 2 + extra)

    def y_copy(t):
        return remote(G.at[p], G.at[p], ygs.at[t], ygr.at[t], (y + t) % Y * 2 + core, c)

    def forward(yy):
        b = yy * 2 + core
        return remote(G.at[b], G.at[b], fws.at[yy], fwr.at[yy], mate, c)

    for t in range(1, Y):
        y_copy(t).start()
    forward(y).start()

    def x_copy(r):
        return remote(
            G.at[p, pl.ds(r * panel, panel)], X.at[p % q], xs.at[r], xr.at[p % q],
            c * ratio + r, p // q,
        )

    for r in range(ratio):
        @pl.when(away(r))
        def _():
            x_copy(r).start()

    def split_root(h, carry):
        rows = pl.ds(pl.multiple_of(h * hr, hr), hr)
        rhi[rows, :], rlo[rows, :] = split(root[rows, :])
        return carry

    lax.fori_loop(0, H, split_root, 0)

    def chain(u, h):
        j = u // q
        rows = pl.ds(pl.multiple_of(h * hr, hr), hr)
        target = jnp.where(j > c, c + 1, c - 1)
        slot = jnp.where((j < c) & (j == c - 1), PR + u % q, u)
        return remote(
            part.at[u, rows], recv.at[slot, rows], chs.at[u, h], chr_.at[slot, h], p, target
        )

    def arrive(slot, h):
        rows = pl.ds(pl.multiple_of(h * hr, hr), hr)
        remote(
            recv.at[slot, rows], recv.at[slot, rows], chs.at[0, h], chr_.at[slot, h], p, c
        ).wait_recv()

    def phase(t, carry):
        yy = (y + Y - t) % Y

        @pl.when(t > 0)
        def _():
            remote(G.at[p], G.at[yy * 2 + core], ygs.at[t], ygr.at[t], p, c).wait_recv()
            forward(yy).start()

        other = yy * 2 + (1 - core)
        remote(G.at[other], G.at[other], fws.at[yy], fwr.at[yy], p, c).wait_recv()
        for i in range(2):
            u = yy * 2 + i

            lhi[i], llo[i] = split(G[u])

        def chunk(h, inner):
            rows = pl.ds(pl.multiple_of(h * hr, hr), hr)
            for i in range(2):
                u = yy * 2 + i
                j = u // q
                part[u, rows, :] = dot3(rhi[rows, :], rlo[rows, :], lhi[i], llo[i])

                @pl.when(((j > c) & (c == 0)) | ((j < c) & (c == PC - 1)))
                def _():
                    chain(u, h).start()

            return inner

        lax.fori_loop(0, H, chunk, 0)
        return carry

    lax.fori_loop(0, Y, phase, 0)

    def relay(h, carry):
        rows = pl.ds(pl.multiple_of(h * hr, hr), hr)

        def unit(u, inner):
            j = u // q

            @pl.when(((j > c) & (c > 0)) | ((j < c) & (c < PC - 1)))
            def _():
                arrive(u, h)
                part[u, rows, :] += recv[u, rows, :]
                chain(u, h).start()

            return inner

        lax.fori_loop(0, PR, unit, 0)
        return carry

    lax.fori_loop(0, H, relay, 0)

    for i in range(q):
        @pl.when((c * q + i == p) & (c == pc))
        def _():
            X[i] = G[c * q + i, pl.ds(row_off, panel), :]

        @pl.when((c * q + i != p) | (c != pc))
        def _():
            remote(X.at[i], X.at[i], xs.at[0], xr.at[i], p, c).wait_recv()

        cols = slice(i * local_cols, (i + 1) * local_cols)
        xthi[cols, :], xtlo[cols, :] = split(X[i].T)

    D[...] = jnp.zeros_like(D)
    for h in range(H):
        rows = slice(h * hr, (h + 1) * hr)
        for i in range(q):
            u = c * q + i

            @pl.when(c > 0)
            def _():
                arrive(u, h)
                part[u, rows, :] += recv[u, rows, :]

            @pl.when(c < PC - 1)
            def _():
                arrive(PR + i, h)
                part[u, rows, :] += recv[PR + i, rows, :]

            cols = slice(i * local_cols, (i + 1) * local_cols)
            done = -part[u, rows, :]
            sel[rows, cols] = done
            D[:, cols] -= dot3(xthi[:, rows], xtlo[:, rows], *split(done))

    share = out.shape[1]

    def d_copy(t):
        pp = (p + t) % PR
        return remote(
            D.at[pl.ds(pl.multiple_of(pp * share, share), share)], E.at[t], ds_.at[t], dr.at[t], pp, c
        )

    for t in range(1, PR):
        d_copy(t).start()
    out[0] = diag[0] + D[pl.ds(pl.multiple_of(p * share, share), share), :]
    for t in range(1, PR):
        d_copy(t).wait_recv()
        out[0] += E[t]

    for t in range(1, PR):
        d_copy(t).wait_send()
    for t in range(1, Y):
        y_copy(t).wait_send()

    def drain_forward(yy, carry):
        forward(yy).wait_send()
        return carry

    lax.fori_loop(0, Y, drain_forward, 0)

    def drain(u, carry):
        @pl.when(u // q != c)
        def _():
            def one(h, inner):
                chain(u, h).wait_send()
                return inner

            lax.fori_loop(0, H, one, 0)

        return carry

    lax.fori_loop(0, PR, drain, 0)
    for r in range(ratio):
        @pl.when(away(r))
        def _():
            x_copy(r).wait_send()


def on_device(PR, PC, root_inverse, lower_blocks, block_pattern, diag_inverse):
    panel, depth = root_inverse.shape
    local_rows, local_cols = lower_blocks.shape
    H = panel // 128
    Y = PR // 2
    owned = local_cols * PR // PC
    q = owned // local_cols
    f32, bf16 = jnp.float32, jnp.bfloat16
    dma = pltpu.SemaphoreType.DMA
    vmem = pl.BlockSpec(memory_space=pltpu.VMEM)
    flops = 6 * panel * depth * local_cols * PR
    return pl.pallas_call(
        functools.partial(kernel, PR, PC, H),
        out_shape=(
            jax.ShapeDtypeStruct((panel, owned), f32),
            jax.ShapeDtypeStruct(diag_inverse.shape, f32),
        ),
        in_specs=[pl.BlockSpec(memory_space=pltpu.SMEM), vmem, vmem, vmem],
        out_specs=(vmem, vmem),
        scratch_shapes=[
            pltpu.VMEM((PR, local_rows, local_cols), f32),
            pltpu.VMEM((PR, panel, local_cols), f32),
            pltpu.VMEM((PR + q, panel, local_cols), f32),
            pltpu.VMEM((panel, depth), bf16),
            pltpu.VMEM((panel, depth), bf16),
            pltpu.VMEM((2, local_rows, local_cols), bf16),
            pltpu.VMEM((2, local_rows, local_cols), bf16),
            pltpu.VMEM((q, panel, local_cols), f32),
            pltpu.VMEM((owned, panel), bf16),
            pltpu.VMEM((owned, panel), bf16),
            pltpu.VMEM((owned, owned), f32),
            pltpu.VMEM((PR,) + diag_inverse.shape[1:], f32),
            dma((Y,)), dma((Y,)), dma((Y,)), dma((Y,)),
            dma((PR, H)), dma((PR + q, H)),
            dma((PR,)), dma((q,)), dma((PR,)), dma((PR,)),
        ],
        compiler_params=pltpu.CompilerParams(
            collective_id=0, has_side_effects=True, vmem_limit_bytes=56 * 1024 * 1024
        ),
        cost_estimate=pl.CostEstimate(flops=flops, bytes_accessed=8 * panel * depth, transcendentals=0),
    )(block_pattern, root_inverse, lower_blocks, diag_inverse)


def solution(mesh):
    placed = (
        P(("pole", "prow"), "pcol"),
        P(("pole", "pcol"), "prow"),
        P(),
        P(("pole", "pcol"), "prow", None),
    )
    return jax.shard_map(
        functools.partial(on_device, mesh.shape["prow"], mesh.shape["pcol"]),
        mesh=mesh,
        in_specs=placed,
        out_specs=(P(("pole", "prow"), "pcol"), P(("pole", "pcol"), "prow", None)),
        check_vma=False,
    )
```

```python
import functools

import jax
import jax.numpy as jnp
from jax import lax
from jax.experimental import pallas as pl
from jax.experimental.pallas import tpu as pltpu
from jax.sharding import PartitionSpec as P

B = 256
MESH = pl.DeviceIdType.MESH


def split(value):
    high = value.astype(jnp.bfloat16)
    return high, (value - high.astype(jnp.float32)).astype(jnp.bfloat16)


def dot3(ahi, alo, bhi, blo):
    dot = functools.partial(jnp.dot, preferred_element_type=jnp.float32)
    return dot(ahi, bhi) + (dot(ahi, blo) + dot(alo, bhi))


def kernel(
    PR, PC, H,
    pattern, root, lower, diag, sel, out,
    G, part, recv, rhi, rlo, lhi, llo, X, xthi, xtlo, D, E,
    ygs, ygr, fws, fwr, chs, chr_, xs, xr, ds_, dr,
):
    x = lax.axis_index("pole")
    p = lax.axis_index("prow")
    c = lax.axis_index("pcol")
    Y = PR // 2
    q = PR // PC if PR > PC else 1
    y, core = p // 2, p % 2
    mate = y * 2 + (1 - core)
    local_rows, local_cols = lower.shape
    panel = root.shape[0]
    hr = panel // H
    ratio = local_rows // panel
    pc = p // ratio
    row_off = pl.multiple_of(p % ratio * panel, panel)

    def remote(src, dst, ss, rs, pp, cc):
        return pltpu.make_async_remote_copy(
            src_ref=src, dst_ref=dst, send_sem=ss, recv_sem=rs,
            device_id=(x, pp, cc), device_id_type=MESH,
        )

    barrier = pltpu.get_barrier_semaphore()
    for t in range(1, PR):
        pl.semaphore_signal(barrier, inc=1, device_id=(x, (p + t) % PR, c), device_id_type=MESH)
    for t in range(1, PC):
        pl.semaphore_signal(barrier, inc=1, device_id=(x, p, (c + t) % PC), device_id_type=MESH)

    def away(r):
        return (c * ratio + r != p) | (p // q != c)

    for r in range(ratio):
        @pl.when(away(r))
        def _():
            pl.semaphore_signal(
                barrier, inc=1, device_id=(x, c * ratio + r, p // q), device_id_type=MESH
            )

    supernode = p * local_cols // B
    for r in range(local_rows // B):
        keep = pattern[c * (local_rows // B) + r, supernode].astype(jnp.float32)
        G[p, r * B:(r + 1) * B, :] = lower[r * B:(r + 1) * B, :] * keep
    extra = sum(jnp.where(away(r), 1, 0) for r in range(ratio))
    pl.semaphore_wait(barrier, PR + PC - 2 + extra)

    def y_copy(t):
        return remote(G.at[p], G.at[p], ygs.at[t], ygr.at[t], (y + t) % Y * 2 + core, c)

    def forward(yy):
        b = yy * 2 + core
        return remote(G.at[b], G.at[b], fws.at[yy], fwr.at[yy], mate, c)

    for t in range(1, Y):
        y_copy(t).start()
    forward(y).start()

    def x_copy(r):
        return remote(
            G.at[p, pl.ds(r * panel, panel)], X.at[p % q], xs.at[r], xr.at[p % q],
            c * ratio + r, p // q,
        )

    def split_root(h, carry):
        rows = pl.ds(pl.multiple_of(h * hr, hr), hr)
        rhi[rows, :], rlo[rows, :] = split(root[rows, :])
        return carry

    lax.fori_loop(0, H, split_root, 0)

    def chain(u, h):
        j = u // q
        rows = pl.ds(pl.multiple_of(h * hr, hr), hr)
        target = jnp.where(j > c, c + 1, c - 1)
        slot = jnp.where((j < c) & (j == c - 1), PR + u % q, u)
        return remote(
            part.at[u, rows], recv.at[slot, rows], chs.at[u, h], chr_.at[slot, h], p, target
        )

    def arrive(slot, h):
        rows = pl.ds(pl.multiple_of(h * hr, hr), hr)
        remote(
            recv.at[slot, rows], recv.at[slot, rows], chs.at[0, h], chr_.at[slot, h], p, c
        ).wait_recv()

    def phase(t, carry):
        yy = (y + Y - t) % Y

        @pl.when(t > 0)
        def _():
            remote(G.at[p], G.at[yy * 2 + core], ygs.at[t], ygr.at[t], p, c).wait_recv()
            forward(yy).start()

        other = yy * 2 + (1 - core)
        remote(G.at[other], G.at[other], fws.at[yy], fwr.at[yy], p, c).wait_recv()
        for i in range(2):
            u = yy * 2 + i

            lhi[i], llo[i] = split(G[u])

        def chunk(h, inner):
            rows = pl.ds(pl.multiple_of(h * hr, hr), hr)
            for i in range(2):
                u = yy * 2 + i
                j = u // q
                part[u, rows, :] = dot3(rhi[rows, :], rlo[rows, :], lhi[i], llo[i])

                @pl.when(((j > c) & (c == 0)) | ((j < c) & (c == PC - 1)))
                def _():
                    chain(u, h).start()

            return inner

        lax.fori_loop(0, H, chunk, 0)
        return carry

    lax.fori_loop(0, Y, phase, 0)

    for r in range(ratio):
        @pl.when(away(r))
        def _():
            x_copy(r).start()

    def relay(h, carry):
        rows = pl.ds(pl.multiple_of(h * hr, hr), hr)

        def unit(u, inner):
            j = u // q

            @pl.when(((j > c) & (c > 0)) | ((j < c) & (c < PC - 1)))
            def _():
                arrive(u, h)
                part[u, rows, :] += recv[u, rows, :]
                chain(u, h).start()

            return inner

        lax.fori_loop(0, PR, unit, 0)
        return carry

    lax.fori_loop(0, H, relay, 0)

    for i in range(q):
        @pl.when((c * q + i == p) & (c == pc))
        def _():
            X[i] = G[c * q + i, pl.ds(row_off, panel), :]

        @pl.when((c * q + i != p) | (c != pc))
        def _():
            remote(X.at[i], X.at[i], xs.at[0], xr.at[i], p, c).wait_recv()

        cols = slice(i * local_cols, (i + 1) * local_cols)
        xthi[cols, :], xtlo[cols, :] = split(X[i].T)

    D[...] = jnp.zeros_like(D)
    for h in range(H):
        rows = slice(h * hr, (h + 1) * hr)
        for i in range(q):
            u = c * q + i

            @pl.when(c > 0)
            def _():
                arrive(u, h)
                part[u, rows, :] += recv[u, rows, :]

            @pl.when(c < PC - 1)
            def _():
                arrive(PR + i, h)
                part[u, rows, :] += recv[PR + i, rows, :]

            cols = slice(i * local_cols, (i + 1) * local_cols)
            done = -part[u, rows, :]
            sel[rows, cols] = done
            D[:, cols] -= dot3(xthi[:, rows], xtlo[:, rows], *split(done))

    share = out.shape[1]

    def d_copy(t):
        pp = (p + t) % PR
        return remote(
            D.at[pl.ds(pl.multiple_of(pp * share, share), share)], E.at[t], ds_.at[t], dr.at[t], pp, c
        )

    for t in range(1, PR):
        d_copy(t).start()
    out[0] = diag[0] + D[pl.ds(pl.multiple_of(p * share, share), share), :]
    for t in range(1, PR):
        d_copy(t).wait_recv()
        out[0] += E[t]

    for t in range(1, PR):
        d_copy(t).wait_send()
    for t in range(1, Y):
        y_copy(t).wait_send()

    def drain_forward(yy, carry):
        forward(yy).wait_send()
        return carry

    lax.fori_loop(0, Y, drain_forward, 0)

    def drain(u, carry):
        @pl.when(u // q != c)
        def _():
            def one(h, inner):
                chain(u, h).wait_send()
                return inner

            lax.fori_loop(0, H, one, 0)

        return carry

    lax.fori_loop(0, PR, drain, 0)
    for r in range(ratio):
        @pl.when(away(r))
        def _():
            x_copy(r).wait_send()


def on_device(PR, PC, root_inverse, lower_blocks, block_pattern, diag_inverse):
    panel, depth = root_inverse.shape
    local_rows, local_cols = lower_blocks.shape
    H = panel // 128
    Y = PR // 2
    owned = local_cols * PR // PC
    q = owned // local_cols
    f32, bf16 = jnp.float32, jnp.bfloat16
    dma = pltpu.SemaphoreType.DMA
    vmem = pl.BlockSpec(memory_space=pltpu.VMEM)
    flops = 6 * panel * depth * local_cols * PR
    return pl.pallas_call(
        functools.partial(kernel, PR, PC, H),
        out_shape=(
            jax.ShapeDtypeStruct((panel, owned), f32),
            jax.ShapeDtypeStruct(diag_inverse.shape, f32),
        ),
        in_specs=[pl.BlockSpec(memory_space=pltpu.SMEM), vmem, vmem, vmem],
        out_specs=(vmem, vmem),
        scratch_shapes=[
            pltpu.VMEM((PR, local_rows, local_cols), f32),
            pltpu.VMEM((PR, panel, local_cols), f32),
            pltpu.VMEM((PR + q, panel, local_cols), f32),
            pltpu.VMEM((panel, depth), bf16),
            pltpu.VMEM((panel, depth), bf16),
            pltpu.VMEM((2, local_rows, local_cols), bf16),
            pltpu.VMEM((2, local_rows, local_cols), bf16),
            pltpu.VMEM((q, panel, local_cols), f32),
            pltpu.VMEM((owned, panel), bf16),
            pltpu.VMEM((owned, panel), bf16),
            pltpu.VMEM((owned, owned), f32),
            pltpu.VMEM((PR,) + diag_inverse.shape[1:], f32),
            dma((Y,)), dma((Y,)), dma((Y,)), dma((Y,)),
            dma((PR, H)), dma((PR + q, H)),
            dma((PR,)), dma((q,)), dma((PR,)), dma((PR,)),
        ],
        compiler_params=pltpu.CompilerParams(
            collective_id=0, has_side_effects=True, vmem_limit_bytes=56 * 1024 * 1024
        ),
        cost_estimate=pl.CostEstimate(flops=flops, bytes_accessed=8 * panel * depth, transcendentals=0),
    )(block_pattern, root_inverse, lower_blocks, diag_inverse)


def solution(mesh):
    placed = (
        P(("pole", "prow"), "pcol"),
        P(("pole", "pcol"), "prow"),
        P(),
        P(("pole", "pcol"), "prow", None),
    )
    return jax.shard_map(
        functools.partial(on_device, mesh.shape["prow"], mesh.shape["pcol"]),
        mesh=mesh,
        in_specs=placed,
        out_specs=(P(("pole", "prow"), "pcol"), P(("pole", "pcol"), "prow", None)),
        check_vma=False,
    )
```
